32 devices in a mesh: groups: 2 (over x), seg: 4 (over z), blk: 4 (over y, core).
Axes of the slice: x: 2, y: 2, z: 4, core: 2. Of those that a mesh axis runs over, the one named last changes fastest.
Arguments:
- base_state: float32 [16, 20, 32, 128], P(('groups', 'seg'), None, 'blk'), parts along dimension 0, may hold values from -6 to 6
- direction: float32 [16, 20, 32, 128], P(('groups', 'seg'), None, 'blk'), parts along dimension 0, may hold values from -6 to 6
- coupling: float32 [40, 20], P('groups'), parts along dimension 0, may hold values from -1.25 to 1.25
- tiles: bfloat16 [8, 32, 16, 128, 128], P('seg', 'blk'), may hold values from -0.15625 to 0.15625
- columns: int32 [8, 32, 16], P('seg', 'blk'), may hold values from 0 to 31, as said below
- wet: int32 [32, 128], P('blk'), may hold values 0 or 1
- basis: float32 [8, 16, 20, 32, 128], P(None, ('groups', 'seg'), None, 'blk'), parts along dimension 1, may hold values from -0.0078125 to 0.0078125
Outputs:
- orthogonal: float32 [16, 20, 32, 128], P(('groups', 'seg'), None, 'blk'), parts along dimension 0
- coefficients: float32 [18], P('groups'), parts along dimension 0
The draws below stay inside these ranges and needn't reach their ends.
There are 2 independent parts, one for each index of `groups`. The reference program is written for one: setup_inputs(seed, part) draws one part's arguments, and reference() takes and returns one part's arrays. A program takes and returns all parts, laid end to end along the dimension named above; an argument that names none is the same for every part. Nothing has to cross between parts.
Inputs may be any that keep to these rules, and one draw needn't show every extreme that they name: columns[s, r, k] = (r + d) mod 32 for some whole d with -2 <= d <= 2; in every segment some entry has d = 2 and some has d = -2.
All inputs are finite; a program needn't handle non-finite values. No bound on the sum of `wet` on one device may be relied on, other than what follows from the above.
Results may differ from the reference program's by a relative error of at most 0.04.
Values may be sent and summed in bfloat16 or wider, within the bound.
A program may use at most 128 MiB of HBM per device.

```python
import jax
import jax.numpy as jnp
from jax import lax

TR = 20
P_SIZE = 128
K = 16
STEPS = 18
KRY = 8
REACH = 2
SEGMENTS = 8
NB = 32


def draw_columns(key, part):
    offsets = jax.random.randint(jax.random.fold_in(key, 11), (SEGMENTS, NB, K), -REACH, REACH + 1)
    offsets = offsets.astype(jnp.int32)
    offsets = offsets.at[:, 0, 0].set(-REACH)
    offsets = offsets.at[:, 1, 0].set(REACH)
    rows = jnp.arange(NB, dtype=jnp.int32)[None, :, None]
    return ((rows + offsets) % NB).astype(jnp.int32)


def set_ends(result, rng, low, top_value):
    extent = result.shape
    spot = [jax.random.randint(jax.random.fold_in(rng, axis), (), 0, extent[axis]) for axis in range(len(extent))]
    result = result.at[tuple(spot)].set(low)
    longest = extent.index(max(extent))
    spot[longest] = (spot[longest] + 1) % extent[longest]
    return result.at[tuple(spot)].set(top_value)


def shard_levels(key, dims, cuts, low, top_value):
    gain = 1.0
    for dim, shards_of in cuts:
        heights = jax.random.uniform(jax.random.fold_in(jax.random.fold_in(key, 6), dim), (shards_of,), jnp.float32, low / len(cuts), top_value / len(cuts))
        gain = gain * jnp.repeat(jnp.exp(heights), dims[dim] // shards_of).reshape((-1,) + (1,) * (len(dims) - 1 - dim))
    return gain


def noise(rng, shape, spread, most, cuts=(), kind=jnp.bfloat16):
    result = jax.random.normal(rng, shape, jnp.float32) * spread
    if len(cuts) > 0:
        result = shard_levels(rng, shape, cuts, -0.22, 0.18) * result
    return jnp.clip(result, min=-most, max=most).astype(kind)


def setup_inputs(seed: int = 0, part: int = 0) -> dict:
    arg_keys = jax.random.split(jax.random.key(seed), 8)
    part_keys = jax.random.split(jax.random.fold_in(arg_keys[7], part), 8)
    base_state = noise(part_keys[0], (SEGMENTS, TR, NB, P_SIZE), 1.0, 6.0, ((0, 4), (2, 4)), jnp.float32)
    direction = noise(part_keys[1], (SEGMENTS, TR, NB, P_SIZE), 1.0, 6.0, ((0, 4), (2, 4)), jnp.float32)
    coupling = noise(part_keys[2], (TR, TR), TR ** -0.5, 1.25, (), jnp.float32)
    tiles = noise(arg_keys[3], (SEGMENTS, NB, K, P_SIZE, P_SIZE), (K * P_SIZE * 5 // 6) ** -0.5, 0.15625, ((0, 4), (1, 4)))
    columns = draw_columns(jax.random.fold_in(arg_keys[7], 71), part)
    wet = set_ends((jax.random.randint(arg_keys[5], (NB, P_SIZE), 0, 4) < 3).astype(jnp.int32), jax.random.fold_in(arg_keys[5], 1), 0, 1)
    basis = noise(part_keys[6], (KRY, SEGMENTS, TR, NB, P_SIZE), (SEGMENTS * TR * NB * P_SIZE) ** -0.5, 0.0078125, ((1, 4), (3, 4)), jnp.float32)
    return {"base_state": base_state, "direction": direction, "coupling": coupling, "tiles": tiles, "columns": columns, "wet": wet, "basis": basis}


def one_segment(items, coupling, wetf):
    state, start, tiles_s, cols_s = items
    slope = 1.0 - jnp.tanh(state) ** 2
    flat = cols_s.reshape(-1).astype(jnp.int32)
    tiles_f = tiles_s.astype(jnp.float32)

    def advance(u, unused):
        source = jnp.einsum('tu,unp->tnp', coupling, slope * u, precision=lax.Precision.HIGHEST)
        drive = (u + 0.5 * source).astype(jnp.bfloat16)
        picked = jnp.take(drive, flat, axis=1).reshape(TR, NB, K, P_SIZE)
        moved = jnp.einsum('rkpq,trkq->trp', tiles_f, picked.astype(jnp.float32))
        return (moved * wetf, None)
    final, unused = lax.scan(advance, start, None, length=STEPS)
    return final

def reference(base_state, direction, coupling, tiles, columns, wet, basis):
    wetf = wet.astype(jnp.float32)
    finals = lax.map(lambda items: one_segment(items, coupling, wetf), (base_state, direction, tiles, columns))
    shot = finals - jnp.roll(direction, -1, axis=0)
    proj = jnp.einsum('jstnp,stnp->j', basis, shot, precision=lax.Precision.HIGHEST)
    orthogonal = shot - jnp.einsum('j,jstnp->stnp', proj, basis, precision=lax.Precision.HIGHEST)
    entries = float(SEGMENTS * TR * NB * P_SIZE)
    length = jnp.sqrt(jnp.sum(orthogonal * orthogonal) / entries)
    return (orthogonal, jnp.concatenate([proj, length[None]]))
```

```python
import functools

import jax
import jax.numpy as jnp
from jax import lax
from jax.experimental import pallas as pl
from jax.experimental.pallas import tpu as pltpu
from jax.sharding import PartitionSpec as P

STEPS = 18
MESH = pl.DeviceIdType.MESH
REACH = 2
PAD = 32


def merge_kernel(total, rows, stored, cols_ref, tiles_ref, w_ref, acc):
    s, g = pl.program_id(0), pl.program_id(1)
    first = lax.axis_index("blk") * rows
    acc[...] = jnp.zeros_like(acc)
    wide = 2 * REACH + 2
    for j in range(2):
        row = 2 * g + j

        def add(k, unused):
            col = cols_ref[(s * rows + row) * stored + k]
            d = lax.rem(col - first - row + (REACH + total), total)
            at = j * wide + j + d
            acc[at] += tiles_ref[0, j, k].astype(jnp.float32)
            return unused

        lax.fori_loop(0, stored, add, 0, unroll=2)
    size = acc.shape[1]
    for j in range(2):
        for c in range(wide):
            w_ref[0, 0, j * size:(j + 1) * size, c * size:(c + 1) * size] = (
                acc[j * wide + c].astype(jnp.bfloat16)
            )


def steps_kernel(
    dims, base_ref, dir_ref, coup_ref, wet_ref, w_hbm, basis_hbm, orth_ref, coef_ref,
    w, basis, drive, slope, cc, wetf, follow, native, part1, part2,
    send_sem, recv_sem, follow_sem, load_sem, red_sem1, red_sem2,
):
    segs, tracers, rows, points, kry, n_seg, n_blk, entries = dims
    pairs = rows // 2
    per = tracers * rows
    me_seg, me_blk = lax.axis_index("seg"), lax.axis_index("blk")
    left, right = lax.rem(me_blk + n_blk - 1, n_blk), lax.rem(me_blk + 1, n_blk)

    w_copy = pltpu.make_async_copy(w_hbm, w, load_sem.at[0])
    basis_copy = pltpu.make_async_copy(basis_hbm, basis, load_sem.at[1])
    w_copy.start()
    basis_copy.start()

    barrier = pltpu.get_barrier_semaphore()
    for i in range(1, n_blk):
        pl.semaphore_signal(barrier, inc=1, device_id={"blk": lax.rem(me_blk + i, n_blk)}, device_id_type=MESH)
    for i in range(1, n_seg):
        pl.semaphore_signal(barrier, inc=1, device_id={"seg": lax.rem(me_seg + i, n_seg)}, device_id_type=MESH)

    c = 0.5 * coup_ref[...]
    high = c.astype(jnp.bfloat16)
    low = (c - high.astype(jnp.float32)).astype(jnp.bfloat16)
    cc[...] = jnp.zeros_like(cc)
    cc[:tracers, 0:tracers] = high.astype(jnp.float32)
    cc[:tracers, PAD:PAD + tracers] = high.astype(jnp.float32)
    cc[:tracers, 2 * PAD:2 * PAD + tracers] = low.astype(jnp.float32)
    mix = cc[...].astype(jnp.bfloat16)
    slope[...] = jnp.zeros_like(slope)
    native[...] = jnp.zeros_like(native)
    for r in range(rows):
        lanes = slice(r * points, (r + 1) * points)
        wetf[:, lanes] = wet_ref[r:r + 1, :].astype(jnp.float32)
        for s in range(segs):
            t = jnp.tanh(base_ref[pl.ds(s * per + r, tracers, stride=rows), :])
            slope[s, :tracers, lanes] = 1.0 - t * t
            native[s, :tracers, lanes] = dir_ref[pl.ds(s * per + r, tracers, stride=rows), :]

    def lanes_of(g, blocks=2):
        return slice(2 * g * points, (2 * g + blocks) * points)

    def force(u, s, g, slot):
        x = slope[s, :, lanes_of(g)] * u
        xh = x.astype(jnp.bfloat16)
        xl = (x - xh.astype(jnp.float32)).astype(jnp.bfloat16)
        stack = jnp.concatenate([xh, xl, xh], axis=0)
        d = u + jnp.dot(mix, stack, preferred_element_type=jnp.float32)
        drive[slot, s, :, lanes_of(g + 1)] = d.astype(jnp.bfloat16)

    def move(s, g, slot):
        m = lax.dot_general(
            drive[slot, s, :, lanes_of(g, 2 * REACH + 2)], w[s, g],
            (((1,), (1,)), ((), ())), preferred_element_type=jnp.float32,
        )
        return m * wetf[:, lanes_of(g)]

    def halos(s, slot):
        return [
            pltpu.make_async_remote_copy(
                src_ref=drive.at[slot, s, :, lanes_of(1)],
                dst_ref=drive.at[slot, s, :, lanes_of(pairs + 1)],
                send_sem=send_sem.at[slot, s, 0], recv_sem=recv_sem.at[slot, s, 0],
                device_id={"blk": left}, device_id_type=MESH,
            ),
            pltpu.make_async_remote_copy(
                src_ref=drive.at[slot, s, :, lanes_of(pairs)],
                dst_ref=drive.at[slot, s, :, lanes_of(0)],
                send_sem=send_sem.at[slot, s, 1], recv_sem=recv_sem.at[slot, s, 1],
                device_id={"blk": right}, device_id_type=MESH,
            ),
        ]

    edges, inner = (0, pairs - 1), range(1, pairs - 1)
    for s in range(segs):
        for g in edges:
            force(native[s, :, lanes_of(g)], s, g, 0)
    pl.semaphore_wait(barrier, n_blk + n_seg - 2)
    for s in range(segs):
        for h in halos(s, 0):
            h.start()
    follow_copy = pltpu.make_async_remote_copy(
        src_ref=dir_ref.at[0:per], dst_ref=follow, send_sem=follow_sem.at[0], recv_sem=follow_sem.at[1],
        device_id={"seg": lax.rem(me_seg + n_seg - 1, n_seg)}, device_id_type=MESH,
    )
    follow_copy.start()
    for s in range(segs):
        for g in inner:
            force(native[s, :, lanes_of(g)], s, g, 0)

    basis_copy.wait()
    chunks = segs * tracers
    half = kry // 2 + 1

    def fold(a):
        return jnp.sum(a, axis=0, keepdims=True)

    def gram(i, acc):
        b = [basis[j, pl.ds(pl.multiple_of(i * rows, rows), rows), :] for j in range(kry)]
        return tuple(acc[m * kry + j] + b[j] * b[(j + m) % kry] for m in range(half) for j in range(kry))

    zero = jnp.zeros((rows, points), jnp.float32)
    sums = lax.fori_loop(0, chunks, gram, (zero,) * (half * kry))
    for m in range(half):
        for j in range(kry):
            part1[me_blk, pl.ds((m + 2) * 8 + j, 1), :] = fold(sums[m * kry + j])

    w_copy.wait()

    def step(slot):
        for s in range(segs):
            for h in halos(s, slot):
                h.wait()
            for g in edges:
                force(move(s, g, slot), s, g, 1 - slot)
            for h in halos(s, 1 - slot):
                h.start()
        for s in range(segs):
            for g in inner:
                force(move(s, g, slot), s, g, 1 - slot)

    def two(i, unused):
        step(0)
        step(1)
        return unused

    lax.fori_loop(0, (STEPS - 1) // 2, two, 0)
    for n in range((STEPS - 1) // 2 * 2, STEPS - 1):
        step(n % 2)
    last = (STEPS - 1) % 2
    for s in range(segs):
        for g in inner:
            native[s, :, lanes_of(g)] = move(s, g, last)
    for s in range(segs):
        for h in halos(s, last):
            h.wait()
        for g in edges:
            native[s, :, lanes_of(g)] = move(s, g, last)
    for s in range(segs):
        for r in range(rows):
            orth_ref[pl.ds(s * per + r, tracers, stride=rows), :] = native[s, :tracers, r * points:(r + 1) * points]
    follow_copy.wait()

    def project(i, acc):
        here = pl.ds(pl.multiple_of(i * rows, rows), rows)
        there = pl.ds(pl.multiple_of(i * rows, rows) + per, rows)
        far = pl.ds(pl.multiple_of(i * rows, rows) + (segs - 1) * per, rows)
        for s in range(segs):
            at = pl.ds(pl.multiple_of(i * rows, rows) + s * per, rows)
            if s < segs - 1:
                nxt = dir_ref[pl.ds(pl.multiple_of(i * rows, rows) + (s + 1) * per, rows), :]
            else:
                nxt = follow[here, :]
            shot = orth_ref[at, :] - nxt
            orth_ref[at, :] = shot
            acc = tuple(acc[j] + basis[j, at, :] * shot for j in range(kry)) + (acc[kry] + shot * shot,)
        return acc

    sums = lax.fori_loop(0, tracers, project, (zero,) * (kry + 1), unroll=4)
    for j in range(kry):
        part1[me_blk, pl.ds(j, 1), :] = fold(sums[j])
    part1[me_blk, pl.ds(8, 8), :] = sums[kry]

    def everyone(part, me, axis, count, sems):
        copies = [
            pltpu.make_async_remote_copy(
                src_ref=part.at[me], dst_ref=part.at[me],
                send_sem=sems.at[0, i - 1], recv_sem=sems.at[1, i - 1],
                device_id={axis: lax.rem(me + i, count)}, device_id_type=MESH,
            )
            for i in range(1, count)
        ]
        for x in copies:
            x.start()
        for x in copies:
            x.wait()
        result = part[0]
        for i in range(1, count):
            result = result + part[i]
        return result

    part2[me_seg] = everyone(part1, me_blk, "blk", n_blk, red_sem1)
    both = everyone(part2, me_seg, "seg", n_seg, red_sem2)
    sumd = jnp.sum(both, axis=1, keepdims=True)
    h = sumd[0:kry]
    hv = [sumd[j:j + 1] for j in range(kry)]
    quad = jnp.zeros((kry, 1), jnp.float32)
    for m in range(half):
        turned = h if m == 0 else jnp.concatenate([h[m:], h[:m]], axis=0)
        weight = 1.0 if m == 0 or 2 * m == kry else 2.0
        quad = quad + weight * (turned * sumd[(m + 2) * 8:(m + 2) * 8 + kry])
    quad = h * (quad - 2.0 * h) + sumd[8:16]
    square = jnp.sum(jnp.broadcast_to(quad, (kry, points)), axis=0, keepdims=True)
    length = jnp.sqrt(jnp.maximum(square, 0.0) / entries)
    coef_ref[kry] = length[0, 0]
    for j in range(kry):
        coef_ref[j] = hv[j][0, 0]
    wide = [jnp.broadcast_to(x, (rows, points)) for x in hv]

    def subtract(i, unused):
        at = pl.ds(pl.multiple_of(i * rows, rows), rows)
        a = hv_sum([wide[j] * basis[j, at, :] for j in range(kry)])
        orth_ref[at, :] = orth_ref[at, :] - a
        return unused

    lax.fori_loop(0, chunks, subtract, 0, unroll=4)


def hv_sum(terms):
    while len(terms) > 1:
        terms = [sum(terms[i:i + 2]) for i in range(0, len(terms), 2)]
    return terms[0]


def on_device(n_seg, n_blk, base_state, direction, coupling, tiles, columns, wet, basis):
    segs, tracers, rows, points = direction.shape
    stored = tiles.shape[2]
    kry = basis.shape[0]
    total = rows * n_blk
    entries = float(segs * n_seg * tracers * total * points)
    pairs = rows // 2
    wide = 2 * REACH + 2
    w = pl.pallas_call(
        functools.partial(merge_kernel, total, rows, stored),
        out_shape=jax.ShapeDtypeStruct((segs, pairs, 2 * points, wide * points), jnp.bfloat16),
        grid_spec=pltpu.PrefetchScalarGridSpec(
            num_scalar_prefetch=1,
            grid=(segs, pairs),
            in_specs=[pl.BlockSpec((1, 2, stored, points, points), lambda s, g, c: (s, g, 0, 0, 0))],
            out_specs=pl.BlockSpec((1, 1, 2 * points, wide * points), lambda s, g, c: (s, g, 0, 0)),
            scratch_shapes=[pltpu.VMEM((2 * wide, points, points), jnp.float32)],
        ),
        compiler_params=pltpu.CompilerParams(vmem_limit_bytes=24 << 20),
        name="merge",
    )(columns.reshape(-1), tiles)
    flat = segs * tracers * rows
    dims = (segs, tracers, rows, points, kry, n_seg, n_blk, entries)
    in_vmem = pl.BlockSpec(memory_space=pltpu.VMEM)
    anywhere = pl.BlockSpec(memory_space=pl.ANY)
    red = (2 + kry // 2 + 1) * 8
    orth, coef = pl.pallas_call(
        functools.partial(steps_kernel, dims),
        out_shape=(
            jax.ShapeDtypeStruct((flat, points), jnp.float32),
            jax.ShapeDtypeStruct((kry + 1,), jnp.float32),
        ),
        in_specs=[in_vmem] * 4 + [anywhere] * 2,
        out_specs=(in_vmem, pl.BlockSpec(memory_space=pltpu.SMEM)),
        scratch_shapes=[
            pltpu.VMEM((segs, pairs, 2 * points, wide * points), jnp.bfloat16),
            pltpu.VMEM((kry, flat, points), jnp.float32),
            pltpu.VMEM((2, segs, PAD, (rows + 2 * REACH) * points), jnp.bfloat16),
            pltpu.VMEM((segs, PAD, rows * points), jnp.float32),
            pltpu.VMEM((PAD, 3 * PAD), jnp.float32),
            pltpu.VMEM((1, rows * points), jnp.float32),
            pltpu.VMEM((tracers * rows, points), jnp.float32),
            pltpu.VMEM((segs, PAD, rows * points), jnp.float32),
            pltpu.VMEM((n_blk, red, points), jnp.float32),
            pltpu.VMEM((n_seg, red, points), jnp.float32),
            pltpu.SemaphoreType.DMA((2, segs, 2)),
            pltpu.SemaphoreType.DMA((2, segs, 2)),
            pltpu.SemaphoreType.DMA((2,)),
            pltpu.SemaphoreType.DMA((2,)),
            pltpu.SemaphoreType.DMA((2, n_blk - 1)),
            pltpu.SemaphoreType.DMA((2, n_seg - 1)),
        ],
        compiler_params=pltpu.CompilerParams(
            collective_id=0, has_side_effects=True, vmem_limit_bytes=40 << 20
        ),
        name="steps",
    )(
        base_state.reshape(flat, points), direction.reshape(flat, points), coupling, wet,
        w, basis.reshape(kry, flat, points),
    )
    return orth.reshape(direction.shape), coef


def solution(mesh):
    in_specs = (
        P(("groups", "seg"), None, "blk", None),
        P(("groups", "seg"), None, "blk", None),
        P("groups", None),
        P("seg", "blk", None, None, None),
        P("seg", "blk", None),
        P("blk", None),
        P(None, ("groups", "seg"), None, "blk", None),
    )
    out_specs = (P(("groups", "seg"), None, "blk", None), P("groups"))
    body = functools.partial(on_device, mesh.shape["seg"], mesh.shape["blk"])
    return jax.shard_map(body, mesh=mesh, in_specs=in_specs, out_specs=out_specs, check_vma=False)
```

```python
import functools

import jax
import jax.numpy as jnp
from jax import lax
from jax.experimental import pallas as pl
from jax.experimental.pallas import tpu as pltpu
from jax.sharding import PartitionSpec as P

STEPS = 18
MESH = pl.DeviceIdType.MESH
REACH = 2
PAD = 32


def merge_kernel(total, rows, stored, cols_ref, tiles_ref, w_ref, acc):
    s, g = pl.program_id(0), pl.program_id(1)
    first = lax.axis_index("blk") * rows
    acc[...] = jnp.zeros_like(acc)
    wide = 2 * REACH + 2
    for j in range(2):
        row = 2 * g + j

        def add(k, unused):
            col = cols_ref[(s * rows + row) * stored + k]
            d = lax.rem(col - first - row + (REACH + total), total)
            at = j * wide + j + d
            acc[at] += tiles_ref[0, j, k].astype(jnp.float32)
            return unused

        lax.fori_loop(0, stored, add, 0, unroll=2)
    size = acc.shape[1]
    for j in range(2):
        for c in range(wide):
            w_ref[0, 0, c * size:(c + 1) * size, j * size:(j + 1) * size] = (
                acc[j * wide + c].T.astype(jnp.bfloat16)
            )


def steps_kernel(
    dims, base_ref, dir_ref, coup_ref, wet_ref, w_hbm, basis_hbm, orth_ref, coef_ref,
    w, basis, drive, slope, cc, wetf, follow, native, part1, part2,
    send_sem, recv_sem, follow_sem, load_sem, red_sem1, red_sem2,
):
    segs, tracers, rows, points, kry, n_seg, n_blk, entries = dims
    pairs = rows // 2
    per = tracers * rows
    me_seg, me_blk = lax.axis_index("seg"), lax.axis_index("blk")
    left, right = lax.rem(me_blk + n_blk - 1, n_blk), lax.rem(me_blk + 1, n_blk)

    w_copy = pltpu.make_async_copy(w_hbm, w, load_sem.at[0])
    basis_copy = pltpu.make_async_copy(basis_hbm, basis, load_sem.at[1])
    w_copy.start()
    basis_copy.start()

    barrier = pltpu.get_barrier_semaphore()
    for i in range(1, n_blk):
        pl.semaphore_signal(barrier, inc=1, device_id={"blk": lax.rem(me_blk + i, n_blk)}, device_id_type=MESH)
    for i in range(1, n_seg):
        pl.semaphore_signal(barrier, inc=1, device_id={"seg": lax.rem(me_seg + i, n_seg)}, device_id_type=MESH)

    c = 0.5 * coup_ref[...]
    high = c.astype(jnp.bfloat16)
    low = (c - high.astype(jnp.float32)).astype(jnp.bfloat16)
    cc[...] = jnp.zeros_like(cc)
    cc[:tracers, 0:tracers] = high.astype(jnp.float32)
    cc[:tracers, PAD:PAD + tracers] = low.astype(jnp.float32)
    mix = cc[...].astype(jnp.bfloat16)
    slope[...] = jnp.zeros_like(slope)
    native[...] = jnp.zeros_like(native)
    for r in range(rows):
        lanes = slice(r * points, (r + 1) * points)
        wetf[:, lanes] = wet_ref[r:r + 1, :].astype(jnp.float32)
        for s in range(segs):
            t = jnp.tanh(base_ref[pl.ds(s * per + r, tracers, stride=rows), :])
            slope[s, :tracers, lanes] = 1.0 - t * t
            native[s, :tracers, lanes] = dir_ref[pl.ds(s * per + r, tracers, stride=rows), :]

    def lanes_of(g, blocks=2):
        return slice(2 * g * points, (2 * g + blocks) * points)

    def force(u, s, g, slot):
        x = slope[s, :, lanes_of(g)] * u
        xh = x.astype(jnp.bfloat16)
        stack = jnp.concatenate([xh, xh], axis=0)
        d = u + jnp.dot(mix, stack, preferred_element_type=jnp.float32)
        drive[slot, s, :, lanes_of(g + 1)] = d.astype(jnp.bfloat16)

    def move(s, g, slot):
        m = jnp.dot(
            drive[slot, s, :, lanes_of(g, 2 * REACH + 2)], w[s, g],
            preferred_element_type=jnp.float32,
        )
        return m * wetf[:, lanes_of(g)]

    def halos(s, slot):
        return [
            pltpu.make_async_remote_copy(
                src_ref=drive.at[slot, s, :, lanes_of(1)],
                dst_ref=drive.at[slot, s, :, lanes_of(pairs + 1)],
                send_sem=send_sem.at[slot, s, 0], recv_sem=recv_sem.at[slot, s, 0],
                device_id={"blk": left}, device_id_type=MESH,
            ),
            pltpu.make_async_remote_copy(
                src_ref=drive.at[slot, s, :, lanes_of(pairs)],
                dst_ref=drive.at[slot, s, :, lanes_of(0)],
                send_sem=send_sem.at[slot, s, 1], recv_sem=recv_sem.at[slot, s, 1],
                device_id={"blk": right}, device_id_type=MESH,
            ),
        ]

    edges, inner = (0, pairs - 1), range(1, pairs - 1)
    for s in range(segs):
        for g in edges:
            force(native[s, :, lanes_of(g)], s, g, 0)
    pl.semaphore_wait(barrier, n_blk + n_seg - 2)
    for s in range(segs):
        for h in halos(s, 0):
            h.start()
    follow_copy = pltpu.make_async_remote_copy(
        src_ref=dir_ref.at[0:per], dst_ref=follow, send_sem=follow_sem.at[0], recv_sem=follow_sem.at[1],
        device_id={"seg": lax.rem(me_seg + n_seg - 1, n_seg)}, device_id_type=MESH,
    )
    follow_copy.start()
    for s in range(segs):
        for g in inner:
            force(native[s, :, lanes_of(g)], s, g, 0)

    basis_copy.wait()
    chunks = segs * tracers
    half = kry // 2 + 1

    def fold(a):
        return jnp.sum(a, axis=0, keepdims=True)

    def gram(i, acc):
        b = [basis[j, pl.ds(pl.multiple_of(i * rows, rows), rows), :] for j in range(kry)]
        return tuple(acc[m * kry + j] + b[j] * b[(j + m) % kry] for m in range(half) for j in range(kry))

    zero = jnp.zeros((rows, points), jnp.float32)
    sums = lax.fori_loop(0, chunks, gram, (zero,) * (half * kry))
    for m in range(half):
        for j in range(kry):
            part1[me_blk, pl.ds((m + 2) * 8 + j, 1), :] = fold(sums[m * kry + j])

    w_copy.wait()

    def step(slot):
        for s in range(segs):
            for h in halos(s, slot):
                h.wait()
            for g in edges:
                force(move(s, g, slot), s, g, 1 - slot)
            for h in halos(s, 1 - slot):
                h.start()
        for s in range(segs):
            for g in inner:
                force(move(s, g, slot), s, g, 1 - slot)

    def two(i, unused):
        step(0)
        step(1)
        return unused

    lax.fori_loop(0, (STEPS - 1) // 2, two, 0)
    for n in range((STEPS - 1) // 2 * 2, STEPS - 1):
        step(n % 2)
    last = (STEPS - 1) % 2
    for s in range(segs):
        for g in inner:
            native[s, :, lanes_of(g)] = move(s, g, last)
    for s in range(segs):
        for h in halos(s, last):
            h.wait()
        for g in edges:
            native[s, :, lanes_of(g)] = move(s, g, last)
    for s in range(segs):
        for r in range(rows):
            orth_ref[pl.ds(s * per + r, tracers, stride=rows), :] = native[s, :tracers, r * points:(r + 1) * points]
    follow_copy.wait()

    def project(i, acc):
        here = pl.ds(pl.multiple_of(i * rows, rows), rows)
        there = pl.ds(pl.multiple_of(i * rows, rows) + per, rows)
        far = pl.ds(pl.multiple_of(i * rows, rows) + (segs - 1) * per, rows)
        for s in range(segs):
            at = pl.ds(pl.multiple_of(i * rows, rows) + s * per, rows)
            if s < segs - 1:
                nxt = dir_ref[pl.ds(pl.multiple_of(i * rows, rows) + (s + 1) * per, rows), :]
            else:
                nxt = follow[here, :]
            shot = orth_ref[at, :] - nxt
            orth_ref[at, :] = shot
            acc = tuple(acc[j] + basis[j, at, :] * shot for j in range(kry)) + (acc[kry] + shot * shot,)
        return acc

    sums = lax.fori_loop(0, tracers, project, (zero,) * (kry + 1), unroll=4)
    for j in range(kry):
        part1[me_blk, pl.ds(j, 1), :] = fold(sums[j])
    part1[me_blk, pl.ds(8, 8), :] = sums[kry]

    def everyone(part, me, axis, count, sems):
        copies = [
            pltpu.make_async_remote_copy(
                src_ref=part.at[me], dst_ref=part.at[me],
                send_sem=sems.at[0, i - 1], recv_sem=sems.at[1, i - 1],
                device_id={axis: lax.rem(me + i, count)}, device_id_type=MESH,
            )
            for i in range(1, count)
        ]
        for x in copies:
            x.start()
        for x in copies:
            x.wait()
        result = part[0]
        for i in range(1, count):
            result = result + part[i]
        return result

    part2[me_seg] = everyone(part1, me_blk, "blk", n_blk, red_sem1)
    both = everyone(part2, me_seg, "seg", n_seg, red_sem2)
    sumd = jnp.sum(both, axis=1, keepdims=True)
    h = sumd[0:kry]
    hv = [sumd[j:j + 1] for j in range(kry)]
    quad = jnp.zeros((kry, 1), jnp.float32)
    for m in range(half):
        turned = h if m == 0 else jnp.concatenate([h[m:], h[:m]], axis=0)
        weight = 1.0 if m == 0 or 2 * m == kry else 2.0
        quad = quad + weight * (turned * sumd[(m + 2) * 8:(m + 2) * 8 + kry])
    quad = h * (quad - 2.0 * h) + sumd[8:16]
    square = jnp.sum(jnp.broadcast_to(quad, (kry, points)), axis=0, keepdims=True)
    length = jnp.sqrt(jnp.maximum(square, 0.0) / entries)
    coef_ref[kry] = length[0, 0]
    for j in range(kry):
        coef_ref[j] = hv[j][0, 0]
    wide = [jnp.broadcast_to(x, (rows, points)) for x in hv]

    def subtract(i, unused):
        at = pl.ds(pl.multiple_of(i * rows, rows), rows)
        a = hv_sum([wide[j] * basis[j, at, :] for j in range(kry)])
        orth_ref[at, :] = orth_ref[at, :] - a
        return unused

    lax.fori_loop(0, chunks, subtract, 0, unroll=4)


def hv_sum(terms):
    while len(terms) > 1:
        terms = [sum(terms[i:i + 2]) for i in range(0, len(terms), 2)]
    return terms[0]


def on_device(n_seg, n_blk, base_state, direction, coupling, tiles, columns, wet, basis):
    segs, tracers, rows, points = direction.shape
    stored = tiles.shape[2]
    kry = basis.shape[0]
    total = rows * n_blk
    entries = float(segs * n_seg * tracers * total * points)
    pairs = rows // 2
    wide = 2 * REACH + 2
    w = pl.pallas_call(
        functools.partial(merge_kernel, total, rows, stored),
        out_shape=jax.ShapeDtypeStruct((segs, pairs, wide * points, 2 * points), jnp.bfloat16),
        grid_spec=pltpu.PrefetchScalarGridSpec(
            num_scalar_prefetch=1,
            grid=(segs, pairs),
            in_specs=[pl.BlockSpec((1, 2, stored, points, points), lambda s, g, c: (s, g, 0, 0, 0))],
            out_specs=pl.BlockSpec((1, 1, wide * points, 2 * points), lambda s, g, c: (s, g, 0, 0)),
            scratch_shapes=[pltpu.VMEM((2 * wide, points, points), jnp.float32)],
        ),
        compiler_params=pltpu.CompilerParams(vmem_limit_bytes=24 << 20),
        name="merge",
    )(columns.reshape(-1), tiles)
    flat = segs * tracers * rows
    dims = (segs, tracers, rows, points, kry, n_seg, n_blk, entries)
    in_vmem = pl.BlockSpec(memory_space=pltpu.VMEM)
    anywhere = pl.BlockSpec(memory_space=pl.ANY)
    red = (2 + kry // 2 + 1) * 8
    orth, coef = pl.pallas_call(
        functools.partial(steps_kernel, dims),
        out_shape=(
            jax.ShapeDtypeStruct((flat, points), jnp.float32),
            jax.ShapeDtypeStruct((kry + 1,), jnp.float32),
        ),
        in_specs=[in_vmem] * 4 + [anywhere] * 2,
        out_specs=(in_vmem, pl.BlockSpec(memory_space=pltpu.SMEM)),
        scratch_shapes=[
            pltpu.VMEM((segs, pairs, wide * points, 2 * points), jnp.bfloat16),
            pltpu.VMEM((kry, flat, points), jnp.float32),
            pltpu.VMEM((2, segs, PAD, (rows + 2 * REACH) * points), jnp.bfloat16),
            pltpu.VMEM((segs, PAD, rows * points), jnp.float32),
            pltpu.VMEM((PAD, 2 * PAD), jnp.float32),
            pltpu.VMEM((1, rows * points), jnp.float32),
            pltpu.VMEM((tracers * rows, points), jnp.float32),
            pltpu.VMEM((segs, PAD, rows * points), jnp.float32),
            pltpu.VMEM((n_blk, red, points), jnp.float32),
            pltpu.VMEM((n_seg, red, points), jnp.float32),
            pltpu.SemaphoreType.DMA((2, segs, 2)),
            pltpu.SemaphoreType.DMA((2, segs, 2)),
            pltpu.SemaphoreType.DMA((2,)),
            pltpu.SemaphoreType.DMA((2,)),
            pltpu.SemaphoreType.DMA((2, n_blk - 1)),
            pltpu.SemaphoreType.DMA((2, n_seg - 1)),
        ],
        compiler_params=pltpu.CompilerParams(
            collective_id=0, has_side_effects=True, vmem_limit_bytes=40 << 20
        ),
        name="steps",
    )(
        base_state.reshape(flat, points), direction.reshape(flat, points), coupling, wet,
        w, basis.reshape(kry, flat, points),
    )
    return orth.reshape(direction.shape), coef


def solution(mesh):
    in_specs = (
        P(("groups", "seg"), None, "blk", None),
        P(("groups", "seg"), None, "blk", None),
        P("groups", None),
        P("seg", "blk", None, None, None),
        P("seg", "blk", None),
        P("blk", None),
        P(None, ("groups", "seg"), None, "blk", None),
    )
    out_specs = (P(("groups", "seg"), None, "blk", None), P("groups"))
    body = functools.partial(on_device, mesh.shape["seg"], mesh.shape["blk"])
    return jax.shard_map(body, mesh=mesh, in_specs=in_specs, out_specs=out_specs, check_vma=False)
```
